512 devices in a mesh: ctx: 64 (over y, z), head: 8 (over x, core).
Axes of the slice: x: 4, y: 8, z: 8, core: 2. Of those that a mesh axis runs over, the one named last changes fastest.
Arguments:
- queries: bfloat16 [32768, 4096], P('ctx', 'head'), may hold values from -6 to 6
- key_vectors: bfloat16 [32768, 4096], P('ctx', 'head'), may hold values from -6 to 6
- value_vectors: bfloat16 [32768, 4096], P('ctx', 'head'), may hold values from -360 to 360
- out_gain: bfloat16 [4096], P('head'), may hold values from 0.099609375 to 1.8984375
- out_grad: bfloat16 [32768, 4096], P('ctx', 'head'), may hold values from -6 to 6
Outputs:
- normed: bfloat16 [32768, 4096], P('ctx', 'head')
- query_grad: bfloat16 [32768, 4096], P('ctx', 'head')
- key_grad: bfloat16 [32768, 4096], P('ctx', 'head')
- value_grad: bfloat16 [32768, 4096], P('ctx', 'head')
The draws below stay inside these ranges and needn't reach their ends.
All inputs are finite; a program needn't handle non-finite values.
Results may differ from the reference program's by a relative error of at most 0.005.
Values sent between devices are 32-bit elements; how exact they have to be, the bound alone decides.
A program may use at most 128 MiB of HBM per device.

```python
import math
import jax
import jax.numpy as jnp
from jax import lax

HEADS = 32
HD = 128
HID = 4096
TOK_DEV = 512
LEN = 32768
N_CTX = 64


def draw_value_vectors(key, part):
    key = jax.random.fold_in(key, 7)
    first_key, second_key = jax.random.split(key, 2)
    column_scale = jnp.exp(jax.random.uniform(second_key, (HID,), jnp.float32, 0.0, math.log(10.0)))
    head_number = (jnp.arange(HID) // HD).astype(jnp.float32)
    base = jnp.clip(jax.random.normal(first_key, (LEN, HID), jnp.float32), -4.0, 4.0)
    rising = 3.0 ** (head_number / (HEADS - 1))
    return (base * column_scale * rising).astype(jnp.bfloat16)


def shard_levels(rng, shape, cuts, smallest, high):
    loudness, own = 1.0, jax.random.fold_in(rng, 6)
    for position, blocks in cuts:
        heights = jnp.exp(jax.random.uniform(jax.random.fold_in(own, position), (blocks,), jnp.float32, smallest / len(cuts), high / len(cuts)))
        loudness = loudness * jnp.repeat(heights, shape[position] // blocks).reshape([-1 if axis == position else 1 for axis in range(len(shape))])
    return loudness


def gaussian(own_key, shape, deviation, bound, cuts=(), held_as=jnp.bfloat16):
    drawn = deviation * jax.random.normal(own_key, shape, jnp.float32)
    if cuts:
        drawn = drawn * shard_levels(own_key, shape, cuts, -0.22, 0.18)
    return jnp.clip(drawn, -bound, bound).astype(held_as)


def setup_inputs(seed: int = 0) -> dict:
    key_list = jax.random.split(jax.random.key(seed), 6)
    queries = gaussian(key_list[0], (LEN, HID), 1.0, 6.0, ((0, 64), (1, 8)))
    key_vectors = gaussian(key_list[1], (LEN, HID), 1.0, 6.0, ((0, 64), (1, 8)))
    value_vectors = draw_value_vectors(jax.random.fold_in(key_list[5], 71), 0)
    out_gain = jnp.clip(1.0 + 0.18 * jax.random.normal(key_list[3], (HID,), jnp.float32), 0.099609375, 1.8984375).astype(jnp.bfloat16)
    out_grad = gaussian(key_list[4], (LEN, HID), 1.0, 6.0, ((0, 64), (1, 8)))
    return {"queries": queries, "key_vectors": key_vectors, "value_vectors": value_vectors, "out_gain": out_gain, "out_grad": out_grad}


epsilon = 1e-05

def reference(queries, key_vectors, value_vectors, out_gain, out_grad):
    score_scale = 1.0 / math.sqrt(HD)
    causal = jnp.tril(jnp.ones((TOK_DEV, TOK_DEV), dtype=bool))

    def split_heads(array):
        return array.reshape(N_CTX, TOK_DEV, HEADS, HD).transpose(2, 0, 1, 3)

    def forward_head(inputs):
        query_all, key_all, value_all = inputs

        def advance(state, block_rows):
            query_rows, key_rows, value_rows = block_rows
            scores = jnp.dot(query_rows, key_rows.T, preferred_element_type=jnp.float32) * score_scale
            weights = jnp.where(causal, scores, 0.0).astype(jnp.bfloat16)
            inner = jnp.dot(weights, value_rows, preferred_element_type=jnp.float32)
            outer = jnp.dot(query_rows.astype(jnp.float32), state, precision=lax.Precision.HIGHEST) * score_scale
            new_state = state + jnp.dot(key_rows.T, value_rows, preferred_element_type=jnp.float32)
            return (new_state, (inner + outer, state))
        start_state = jnp.zeros((HD, HD), jnp.float32)
        unused, results = lax.scan(advance, start_state, (query_all, key_all, value_all))
        return results
    query_heads = split_heads(queries)
    key_heads = split_heads(key_vectors)
    value_heads = split_heads(value_vectors)
    attended, priors = lax.map(forward_head, (query_heads, key_heads, value_heads))
    gain_full = out_gain.astype(jnp.float32).reshape(HEADS, 1, 1, HD)
    grad_in = gain_full * split_heads(out_grad).astype(jnp.float32)
    squares = lax.optimization_barrier(jnp.sum(attended * attended, axis=(0, 3)))
    crossed = lax.optimization_barrier(jnp.sum(grad_in * attended, axis=(0, 3)))
    inverse_rms = lax.rsqrt(squares / HID + epsilon)[None, :, :, None]
    mean_cross = (crossed / HID)[None, :, :, None]
    normed = (attended * inverse_rms * gain_full).astype(jnp.bfloat16)
    grad_out = (inverse_rms * grad_in - attended * (inverse_rms * inverse_rms * inverse_rms * mean_cross)).astype(jnp.bfloat16)

    def backward_head(inputs):
        query_all, key_all, value_all, grad_all, prior_all = inputs

        def retreat(later, block_rows):
            query_rows, key_rows, value_rows, grad_rows, prior = block_rows
            scores = jnp.dot(query_rows, key_rows.T, preferred_element_type=jnp.float32) * score_scale
            weights = jnp.where(causal, scores, 0.0).astype(jnp.bfloat16)
            dscores = jnp.dot(grad_rows, value_rows.T, preferred_element_type=jnp.float32) * score_scale
            dweights = jnp.where(causal, dscores, 0.0).astype(jnp.bfloat16)
            query_part = jnp.dot(dweights, key_rows, preferred_element_type=jnp.float32) + jnp.dot(grad_rows.astype(jnp.float32), prior.T, precision=lax.Precision.HIGHEST) * score_scale
            key_part = jnp.dot(dweights.T, query_rows, preferred_element_type=jnp.float32) + jnp.dot(value_rows.astype(jnp.float32), later.T, precision=lax.Precision.HIGHEST) * score_scale
            value_part = jnp.dot(weights.T, grad_rows, preferred_element_type=jnp.float32) + jnp.dot(key_rows.astype(jnp.float32), later, precision=lax.Precision.HIGHEST) * score_scale
            new_later = later + jnp.dot(query_rows.T, grad_rows, preferred_element_type=jnp.float32)
            return (new_later, (query_part.astype(jnp.bfloat16), key_part.astype(jnp.bfloat16), value_part.astype(jnp.bfloat16)))
        start_state = jnp.zeros((HD, HD), jnp.float32)
        unused, results = lax.scan(retreat, start_state, (query_all, key_all, value_all, grad_all, prior_all), reverse=True)
        return results
    query_grad, key_grad, value_grad = lax.map(backward_head, (query_heads, key_heads, value_heads, grad_out, priors))

    def merge_heads(array):
        return array.transpose(1, 2, 0, 3).reshape(LEN, HID)
    return (merge_heads(normed), merge_heads(query_grad), merge_heads(key_grad), merge_heads(value_grad))
```

```python
import functools
import math

import jax
import jax.numpy as jnp
from jax import lax
from jax.experimental import pallas as pl
from jax.experimental.pallas import tpu as pltpu
from jax.sharding import PartitionSpec as P

HD = 128
TOK = 512
HEADS_HERE = 4
NZ = 8
EPSILON = 1e-05
SCALE = 1.0 / math.sqrt(HD)
MESH = pl.DeviceIdType.MESH
F32 = jnp.float32
BF16 = jnp.bfloat16


def product(a, b, contract):
    return lax.dot_general(a, b, ((contract[:1], contract[1:]), ((), ())), preferred_element_type=F32)


def rows_by_rows(a, b):
    return product(a, b, (1, 1))


def plain(a, b):
    return product(a, b, (1, 0))


def two_terms(state):
    high = state.astype(BF16)
    return high, (state - high.astype(F32)).astype(BF16)


def by_state(rows, state):
    high, low = two_terms(state)
    return plain(jnp.concatenate([rows, rows], axis=1), jnp.concatenate([high, low], axis=0)) * SCALE


def by_state_transposed(rows, state):
    high, low = two_terms(state)
    return rows_by_rows(jnp.concatenate([rows, rows], axis=1), jnp.concatenate([high, low], axis=1)) * SCALE


def score_block(a, b, keep):
    scores = rows_by_rows(a, b) * SCALE
    if keep is not None:
        scores = jnp.where(keep, scores, 0.0)
    return scores.astype(BF16)


def half_masks():
    half = TOK // 2
    rows = lax.broadcasted_iota(jnp.int32, (half, half), 0)
    columns = lax.broadcasted_iota(jnp.int32, (half, half), 1)
    return rows >= columns, rows <= columns


def sum_before(a, b, c, keep):
    half = TOK // 2
    first = plain(score_block(a[:half], b[:half], keep), c[:half])
    weights = jnp.concatenate([score_block(a[half:], b[:half], None), score_block(a[half:], b[half:], keep)], axis=1)
    return jnp.concatenate([first, plain(weights, c)], axis=0)


def sum_after(a, b, c, keep):
    half = TOK // 2
    weights = jnp.concatenate([score_block(a[:half], b[:half], keep), score_block(a[:half], b[half:], None)], axis=1)
    last = plain(score_block(a[half:], b[half:], keep), c[half:])
    return jnp.concatenate([plain(weights, c), last], axis=0)


def each_head(body):
    lax.fori_loop(0, HEADS_HERE, lambda h, _: (body(h), 0)[1], 0)


def attention_kernel(
    n_y, n_head,
    q_hbm, k_hbm, v_hbm, g_hbm, gain_ref,
    normed_ref, query_grad_ref, key_grad_ref, value_grad_ref,
    q, k, v, g, attended, inner_key, inner_value, do, prior, later,
    own, parts, totals, prefixes, total_out, sums, sums_out,
    in_sem, send_sem, recv_sem, sums_send, sums_recv,
):
    place, lane = lax.axis_index("ctx"), lax.axis_index("head")
    y, z = place // NZ, lax.rem(place, NZ)

    def along_z(other):
        return (y * NZ + other, lane)

    def along_y(other):
        return (other * NZ + z, lane)

    def along_head(other):
        return (place, other)

    def others(me, count):
        middle = count // 2
        steps = sorted(range(1, count), key=lambda step: (abs(step - middle), step))
        return [lax.rem(me + step, count) for step in steps]

    barrier = pltpu.get_barrier_semaphore()
    for me, count, device in ((z, NZ, along_z), (y, n_y, along_y), (lane, n_head, along_head)):
        for other in others(me, count):
            pl.semaphore_signal(barrier, inc=1, device_id=device(other), device_id_type=MESH)

    loads = []
    for source, target in ((k_hbm, k), (v_hbm, v), (q_hbm, q), (g_hbm, g)):
        loads.append([
            pltpu.make_async_copy(
                source.at[:, pl.ds(h * HD, HD)], target.at[h], in_sem.at[len(loads), h]
            )
            for h in range(HEADS_HERE)
        ])
    for pair in ((0, 1), (2, 3)):
        for h in range(HEADS_HERE):
            for which in pair:
                loads[which][h].start()

    def wait_all(phase, h, buffer, count):
        whole = buffer.at[h, pl.ds(0, count)]
        pltpu.make_async_remote_copy(
            src_ref=whole, dst_ref=whole, send_sem=send_sem.at[phase, h], recv_sem=recv_sem.at[phase, h],
            device_id=(place, lane), device_id_type=MESH,
        ).wait_recv()

    def wait_sent(phase, h, buffer, count):
        whole = buffer.at[h, pl.ds(0, count)]
        pltpu.make_async_remote_copy(
            src_ref=whole, dst_ref=whole, send_sem=send_sem.at[phase, h], recv_sem=recv_sem.at[phase, h],
            device_id=(place, lane), device_id_type=MESH,
        ).wait_send()

    def give_parts(scan, h):
        for other in others(z, NZ):
            pltpu.make_async_remote_copy(
                src_ref=own.at[scan, h, other], dst_ref=parts.at[scan, h, z],
                send_sem=send_sem.at[3 * scan, h], recv_sem=recv_sem.at[3 * scan, h],
                device_id=along_z(other), device_id_type=MESH,
            ).start()
        parts[scan, h, z] = own[scan, h, z]

    def give_totals(scan, h):
        wait_all(3 * scan, h, parts.at[scan], NZ - 1)
        running = jnp.zeros(parts.shape[3:], F32)
        for at in range(NZ) if scan == 0 else reversed(range(NZ)):
            prefixes[scan, h, at] = running
            running = running + parts[scan, h, at]
        total_out[scan, h] = running
        for other in others(y, n_y):
            pltpu.make_async_remote_copy(
                src_ref=total_out.at[scan, h], dst_ref=totals.at[scan, h, y],
                send_sem=send_sem.at[3 * scan + 1, h], recv_sem=recv_sem.at[3 * scan + 1, h],
                device_id=along_y(other), device_id_type=MESH,
            ).start()
        totals[scan, h, y] = running

    def give_prefixes(scan, h, state):
        wait_all(3 * scan + 1, h, totals.at[scan], n_y - 1)
        offset = jnp.zeros(parts.shape[3:], F32)
        for at in range(n_y) if scan == 0 else reversed(range(n_y)):
            reached = at < y if scan == 0 else at > y
            offset = jnp.where(reached, offset + totals[scan, h, at], offset)
        for at in range(NZ):
            prefixes[scan, h, at] = prefixes[scan, h, at] + offset
        for other in others(z, NZ):
            pltpu.make_async_remote_copy(
                src_ref=prefixes.at[scan, h, other], dst_ref=state.at[h, z],
                send_sem=send_sem.at[3 * scan + 2, h], recv_sem=recv_sem.at[3 * scan + 2, h],
                device_id=along_z(other), device_id_type=MESH,
            ).start()
        state[h, z] = prefixes[scan, h, z]

    def whole_state(scan, h, state):
        wait_all(3 * scan + 2, h, state, NZ - 1)
        return state[h].reshape(HD, HD)

    below, above = half_masks()

    for h in range(HEADS_HERE):
        loads[0][h].wait()
        loads[1][h].wait()
        own[0, h] = product(k[h], v[h], (0, 0)).reshape(own.shape[2:])
        if h == 0:
            pl.semaphore_wait(barrier, NZ + n_y + n_head - 3)
        give_parts(0, h)

    for h in range(HEADS_HERE):
        loads[2][h].wait()
        loads[3][h].wait()

    def inner_products(h):
        attended[h] = sum_before(q[h], k[h], v[h], below)

    each_head(inner_products)
    for h in range(HEADS_HERE):
        give_totals(0, h)
    for h in range(HEADS_HERE):
        give_prefixes(0, h, prior)

    squares = jnp.zeros((TOK, HD), F32)
    crossed = jnp.zeros((TOK, HD), F32)
    gains = [gain_ref[:, pl.ds(h * HD, HD)].astype(F32) for h in range(HEADS_HERE)]
    for h in range(HEADS_HERE):
        rows = attended[h] + by_state(q[h], whole_state(0, h, prior))
        attended[h] = rows
        squares = squares + rows * rows
        crossed = crossed + gains[h] * g[h].astype(F32) * rows

    ones = jnp.ones((8, HD), F32)
    row = lax.broadcasted_iota(jnp.int32, (8, HD), 0)
    packed = jnp.zeros((8, HD), F32)
    for first, array in ((0, squares), (4, crossed)):
        by_token = lax.dot_general(
            ones, array, (((1,), (1,)), ((), ())), precision=lax.Precision.HIGHEST, preferred_element_type=F32
        )
        for r in range(4):
            packed = jnp.where(row == first + r, by_token[:, r * HD : (r + 1) * HD], packed)
    sums_out[...] = packed
    for other in others(lane, n_head):
        pltpu.make_async_remote_copy(
            src_ref=sums_out, dst_ref=sums.at[lane], send_sem=sums_send, recv_sem=sums_recv,
            device_id=along_head(other), device_id_type=MESH,
        ).start()
    sums[lane] = packed
    arrived = sums.at[pl.ds(0, n_head - 1)]
    sums_wait = pltpu.make_async_remote_copy(
        src_ref=arrived, dst_ref=arrived, send_sem=sums_send, recv_sem=sums_recv,
        device_id=(place, lane), device_id_type=MESH,
    )
    sums_wait.wait_recv()
    total = sums[0]
    for at in range(1, n_head):
        total = total + sums[at]
    mean = total * (1.0 / (n_head * HEADS_HERE * HD))
    inverse_rms = lax.rsqrt(mean + EPSILON)
    cubed = inverse_rms * inverse_rms * inverse_rms
    cross_factor = pltpu.roll(cubed, 4, 0) * mean
    factors = jnp.where(row < 4, inverse_rms, cross_factor)
    columns = jnp.concatenate([factors] * (HD // 8), axis=0).T
    rms_column = jnp.concatenate([columns[:, r : r + 1] for r in range(4)], axis=0)
    cross_column = jnp.concatenate([columns[:, 4 + r : 5 + r] for r in range(4)], axis=0)

    for h in range(HEADS_HERE):
        grad_in = gains[h] * g[h].astype(F32)
        do[h] = (rms_column * grad_in - attended[h] * cross_column).astype(BF16)
        own[1, h] = product(q[h], do[h], (0, 0)).reshape(own.shape[2:])
        give_parts(1, h)

    for h in range(HEADS_HERE):
        normed_ref[h] = (attended[h] * rms_column * gains[h]).astype(BF16)

    def query_products(h):
        inner = sum_before(do[h], v[h], k[h], below)
        query_grad_ref[h] = (inner + by_state_transposed(do[h], prior[h].reshape(HD, HD))).astype(BF16)

    each_head(query_products)
    for h in range(HEADS_HERE):
        give_totals(1, h)

    def key_products(h):
        inner_key[h] = sum_after(v[h], do[h], q[h], above)
        inner_value[h] = sum_after(k[h], q[h], do[h], above)

    each_head(key_products)
    for h in range(HEADS_HERE):
        give_prefixes(1, h, later)
    for h in range(HEADS_HERE):
        state = whole_state(1, h, later)
        key_grad_ref[h] = (inner_key[h] + by_state_transposed(v[h], state)).astype(BF16)
        value_grad_ref[h] = (inner_value[h] + by_state(k[h], state)).astype(BF16)

    sums_wait.wait_send()
    for scan in range(2):
        for h in range(HEADS_HERE):
            wait_sent(3 * scan, h, parts.at[scan], NZ - 1)
            wait_sent(3 * scan + 1, h, totals.at[scan], n_y - 1)
            wait_sent(3 * scan + 2, h, prior, NZ - 1)


def store_kernel(*refs):
    sources, targets, sem = refs[:4], refs[4:8], refs[8]
    copies = [
        pltpu.make_async_copy(source.at[h], target.at[:, pl.ds(h * HD, HD)], sem.at[i, h])
        for i, (source, target) in enumerate(zip(sources, targets))
        for h in range(HEADS_HERE)
    ]
    for copy in copies:
        copy.start()
    for copy in copies:
        copy.wait()


def shards(n_y, n_head, queries, key_vectors, value_vectors, out_gain, out_grad):
    part = HD // NZ
    by_head = (HEADS_HERE, TOK, HD)
    state = (HEADS_HERE, NZ, part, HD)
    anywhere = pl.BlockSpec(memory_space=pl.ANY)
    vmem = pl.BlockSpec(memory_space=pltpu.VMEM)
    results = pl.pallas_call(
        functools.partial(attention_kernel, n_y, n_head),
        out_shape=[pltpu.VMEM(by_head, BF16)] * 4,
        in_specs=[anywhere] * 4 + [vmem],
        out_specs=[vmem] * 4,
        scratch_shapes=[pltpu.VMEM(by_head, BF16)] * 4
        + [pltpu.VMEM(by_head, F32)] * 3
        + [
            pltpu.VMEM(by_head, BF16),
            pltpu.VMEM(state, F32),
            pltpu.VMEM(state, F32),
            pltpu.VMEM((2,) + state, F32),
            pltpu.VMEM((2,) + state, F32),
            pltpu.VMEM((2, HEADS_HERE, n_y, part, HD), F32),
            pltpu.VMEM((2,) + state, F32),
            pltpu.VMEM((2, HEADS_HERE, part, HD), F32),
            pltpu.VMEM((n_head, 8, HD), F32),
            pltpu.VMEM((8, HD), F32),
            pltpu.SemaphoreType.DMA((4, HEADS_HERE)),
            pltpu.SemaphoreType.DMA((6, HEADS_HERE)),
            pltpu.SemaphoreType.DMA((6, HEADS_HERE)),
            pltpu.SemaphoreType.DMA,
            pltpu.SemaphoreType.DMA,
        ],
        compiler_params=pltpu.CompilerParams(
            collective_id=0, has_side_effects=True, vmem_limit_bytes=32 * 2**20
        ),
        name="attention",
    )(queries, key_vectors, value_vectors, out_grad, out_gain.reshape(1, HEADS_HERE * HD))
    whole = jax.ShapeDtypeStruct((TOK, HEADS_HERE * HD), BF16)
    return pl.pallas_call(
        store_kernel,
        out_shape=[whole] * 4,
        in_specs=[vmem] * 4,
        out_specs=[anywhere] * 4,
        scratch_shapes=[pltpu.SemaphoreType.DMA((4, HEADS_HERE))],
        name="store",
    )(*results)


def solution(mesh):
    n_y, n_head = mesh.shape["ctx"] // NZ, mesh.shape["head"]
    spec = P("ctx", "head")
    return jax.shard_map(
        functools.partial(shards, n_y, n_head),
        mesh=mesh,
        in_specs=(spec, spec, spec, P("head"), spec),
        out_specs=(spec,) * 4,
        check_vma=False,
    )
```

```python
import functools
import math

import jax
import jax.numpy as jnp
from jax import lax
from jax.experimental import pallas as pl
from jax.experimental.pallas import tpu as pltpu
from jax.sharding import PartitionSpec as P

HD = 128
TOK = 512
HEADS_HERE = 4
NZ = 8
EPSILON = 1e-05
SCALE = 1.0 / math.sqrt(HD)
MESH = pl.DeviceIdType.MESH
F32 = jnp.float32
BF16 = jnp.bfloat16


def product(a, b, contract):
    return lax.dot_general(a, b, ((contract[:1], contract[1:]), ((), ())), preferred_element_type=F32)


def rows_by_rows(a, b):
    return product(a, b, (1, 1))


def plain(a, b):
    return product(a, b, (1, 0))


def two_terms(state):
    high = state.astype(BF16)
    return high, (state - high.astype(F32)).astype(BF16)


def by_state(rows, state):
    high, low = two_terms(state)
    return plain(jnp.concatenate([rows, rows], axis=1), jnp.concatenate([high, low], axis=0)) * SCALE


def by_state_transposed(rows, state):
    high, low = two_terms(state)
    return rows_by_rows(jnp.concatenate([rows, rows], axis=1), jnp.concatenate([high, low], axis=1)) * SCALE


def score_block(a, b, keep):
    scores = rows_by_rows(a, b) * SCALE
    if keep is not None:
        scores = jnp.where(keep, scores, 0.0)
    return scores.astype(BF16)


def half_masks():
    half = TOK // 2
    rows = lax.broadcasted_iota(jnp.int32, (half, half), 0)
    columns = lax.broadcasted_iota(jnp.int32, (half, half), 1)
    return rows >= columns, rows <= columns


def sum_before(a, b, c, keep):
    half = TOK // 2
    first = plain(score_block(a[:half], b[:half], keep), c[:half])
    weights = jnp.concatenate([score_block(a[half:], b[:half], None), score_block(a[half:], b[half:], keep)], axis=1)
    return jnp.concatenate([first, plain(weights, c)], axis=0)


def sum_after(a, b, c, keep):
    half = TOK // 2
    weights = jnp.concatenate([score_block(a[:half], b[:half], keep), score_block(a[:half], b[half:], None)], axis=1)
    last = plain(score_block(a[half:], b[half:], keep), c[half:])
    return jnp.concatenate([plain(weights, c), last], axis=0)


def columns_of(h):
    return pl.ds(h * HD if isinstance(h, int) else pl.multiple_of(h * HD, HD), HD)


def each_head(body):
    lax.fori_loop(0, HEADS_HERE, lambda h, _: (body(h), 0)[1], 0)


def attention_kernel(
    n_y, n_head,
    q_hbm, k_hbm, v_hbm, g_hbm, gain_hbm,
    normed_ref, query_grad_ref, key_grad_ref, value_grad_ref,
    q, k, v, g, gain, attended, inner_key, inner_value, do, prior, later,
    own, parts, totals, prefixes, total_out, sums, sums_out,
    in_sem, gain_sem, send_sem, recv_sem, sums_send, sums_recv,
):
    place, lane = lax.axis_index("ctx"), lax.axis_index("head")
    y, z = place // NZ, lax.rem(place, NZ)

    def along_z(other):
        return (y * NZ + other, lane)

    def along_y(other):
        return (other * NZ + z, lane)

    def along_head(other):
        return (place, other)

    def others(me, count):
        middle = count // 2
        steps = sorted(range(1, count), key=lambda step: (abs(step - middle), step))
        return [lax.rem(me + step, count) for step in steps]

    barrier = pltpu.get_barrier_semaphore()
    for me, count, device in ((z, NZ, along_z), (y, n_y, along_y), (lane, n_head, along_head)):
        for other in others(me, count):
            pl.semaphore_signal(barrier, inc=1, device_id=device(other), device_id_type=MESH)

    loads = []
    for source, target in ((k_hbm, k), (v_hbm, v), (q_hbm, q), (g_hbm, g)):
        loads.append([
            pltpu.make_async_copy(
                source.at[:, pl.ds(h * HD, HD)], target.at[h], in_sem.at[len(loads), h]
            )
            for h in range(HEADS_HERE)
        ])
    gain_load = pltpu.make_async_copy(gain_hbm, gain, gain_sem)
    for pair in ((0, 1), (2, 3)):
        for h in range(HEADS_HERE):
            for which in pair:
                loads[which][h].start()
    gain_load.start()

    def wait_all(phase, h, buffer, count):
        whole = buffer.at[h, pl.ds(0, count)]
        pltpu.make_async_remote_copy(
            src_ref=whole, dst_ref=whole, send_sem=send_sem.at[phase, h], recv_sem=recv_sem.at[phase, h],
            device_id=(place, lane), device_id_type=MESH,
        ).wait_recv()

    def wait_sent(phase, h, buffer, count):
        whole = buffer.at[h, pl.ds(0, count)]
        pltpu.make_async_remote_copy(
            src_ref=whole, dst_ref=whole, send_sem=send_sem.at[phase, h], recv_sem=recv_sem.at[phase, h],
            device_id=(place, lane), device_id_type=MESH,
        ).wait_send()

    def give_parts(scan, h):
        for other in others(z, NZ):
            pltpu.make_async_remote_copy(
                src_ref=own.at[scan, h, other], dst_ref=parts.at[scan, h, z],
                send_sem=send_sem.at[3 * scan, h], recv_sem=recv_sem.at[3 * scan, h],
                device_id=along_z(other), device_id_type=MESH,
            ).start()
        parts[scan, h, z] = own[scan, h, z]

    def give_totals(scan, h):
        wait_all(3 * scan, h, parts.at[scan], NZ - 1)
        order = list(range(NZ)) if scan == 0 else list(reversed(range(NZ)))
        running = parts[scan, h, order[0]]
        for at in order[1:]:
            running = running + parts[scan, h, at]
        total_out[scan, h] = running
        for other in others(y, n_y):
            pltpu.make_async_remote_copy(
                src_ref=total_out.at[scan, h], dst_ref=totals.at[scan, h, y],
                send_sem=send_sem.at[3 * scan + 1, h], recv_sem=recv_sem.at[3 * scan + 1, h],
                device_id=along_y(other), device_id_type=MESH,
            ).start()
        totals[scan, h, y] = running
        running = jnp.zeros(parts.shape[3:], F32)
        for at in order:
            prefixes[scan, h, at] = running
            running = running + parts[scan, h, at]

    def give_prefixes(scan, h, state):
        wait_all(3 * scan + 1, h, totals.at[scan], n_y - 1)
        offset = jnp.zeros(parts.shape[3:], F32)
        for at in range(n_y) if scan == 0 else reversed(range(n_y)):
            reached = at < y if scan == 0 else at > y
            offset = jnp.where(reached, offset + totals[scan, h, at], offset)
        for at in range(NZ):
            prefixes[scan, h, at] = prefixes[scan, h, at] + offset
        for other in others(z, NZ) if scan == 0 else others(z, NZ):
            pltpu.make_async_remote_copy(
                src_ref=prefixes.at[scan, h, other], dst_ref=state.at[h, z],
                send_sem=send_sem.at[3 * scan + 2, h], recv_sem=recv_sem.at[3 * scan + 2, h],
                device_id=along_z(other), device_id_type=MESH,
            ).start()
        state[h, z] = prefixes[scan, h, z]

    def whole_state(scan, h, state):
        wait_all(3 * scan + 2, h, state, NZ - 1)
        return state[h].reshape(HD, HD)

    below, above = half_masks()

    for h in range(HEADS_HERE):
        loads[0][h].wait()
        loads[1][h].wait()
        own[0, h] = product(k[h], v[h], (0, 0)).reshape(own.shape[2:])
        if h == 0:
            pl.semaphore_wait(barrier, NZ + n_y + n_head - 3)
        give_parts(0, h)

    for h in range(HEADS_HERE):
        loads[2][h].wait()
        loads[3][h].wait()
    gain_load.wait()

    def inner_products(h):
        attended[h] = sum_before(q[h], k[h], v[h], below)

    each_head(inner_products)
    for h in range(HEADS_HERE):
        give_totals(0, h)
    for h in range(HEADS_HERE):
        give_prefixes(0, h, prior)

    squares = jnp.zeros((TOK, HD), F32)
    crossed = jnp.zeros((TOK, HD), F32)
    gains = [gain[pl.ds(h * HD, HD)].astype(F32).reshape(1, HD) for h in range(HEADS_HERE)]
    for h in range(HEADS_HERE):
        rows = attended[h] + by_state(q[h], whole_state(0, h, prior))
        attended[h] = rows
        squares = squares + rows * rows
        crossed = crossed + gains[h] * g[h].astype(F32) * rows

    ones = jnp.ones((8, HD), F32)
    row = lax.broadcasted_iota(jnp.int32, (8, HD), 0)
    packed = jnp.zeros((8, HD), F32)
    for first, array in ((0, squares), (4, crossed)):
        by_token = lax.dot_general(
            ones, array, (((1,), (1,)), ((), ())), precision=lax.Precision.HIGHEST, preferred_element_type=F32
        )
        for r in range(4):
            packed = jnp.where(row == first + r, by_token[:, r * HD : (r + 1) * HD], packed)
    sums_out[...] = packed
    for other in others(lane, n_head):
        pltpu.make_async_remote_copy(
            src_ref=sums_out, dst_ref=sums.at[lane], send_sem=sums_send, recv_sem=sums_recv,
            device_id=along_head(other), device_id_type=MESH,
        ).start()
    sums[lane] = packed
    arrived = sums.at[pl.ds(0, n_head - 1)]
    sums_wait = pltpu.make_async_remote_copy(
        src_ref=arrived, dst_ref=arrived, send_sem=sums_send, recv_sem=sums_recv,
        device_id=(place, lane), device_id_type=MESH,
    )
    sums_wait.wait_recv()
    total = sums[0]
    for at in range(1, n_head):
        total = total + sums[at]
    mean = total * (1.0 / (n_head * HEADS_HERE * HD))
    inverse_rms = lax.rsqrt(mean + EPSILON)
    cubed = inverse_rms * inverse_rms * inverse_rms
    cross_factor = pltpu.roll(cubed, 4, 0) * mean
    factors = jnp.where(row < 4, inverse_rms, cross_factor)
    columns = jnp.concatenate([factors] * (HD // 8), axis=0).T
    rms_column = jnp.concatenate([columns[:, r : r + 1] for r in range(4)], axis=0)
    cross_column = jnp.concatenate([columns[:, 4 + r : 5 + r] for r in range(4)], axis=0)

    for h in range(HEADS_HERE):
        grad_in = gains[h] * g[h].astype(F32)
        do[h] = (rms_column * grad_in - attended[h] * cross_column).astype(BF16)
        own[1, h] = product(q[h], do[h], (0, 0)).reshape(own.shape[2:])
        give_parts(1, h)

    for h in range(HEADS_HERE):
        normed_ref[:, columns_of(h)] = (attended[h] * rms_column * gains[h]).astype(BF16)

    def query_products(h):
        inner = sum_before(do[h], v[h], k[h], below)
        query_grad_ref[:, columns_of(h)] = (inner + by_state_transposed(do[h], prior[h].reshape(HD, HD))).astype(BF16)

    each_head(query_products)

    def key_products(h):
        inner_key[h] = sum_after(v[h], do[h], q[h], above)
        inner_value[h] = sum_after(k[h], q[h], do[h], above)

    for h in range(HEADS_HERE):
        give_totals(1, h)
        key_products(h)
    for scan in range(2):
        for h in range(HEADS_HERE):
            wait_sent(3 * scan, h, parts.at[scan], NZ - 1)
    for h in range(HEADS_HERE):
        wait_sent(1, h, totals.at[0], n_y - 1)
        wait_sent(2, h, prior, NZ - 1)
    sums_wait.wait_send()
    for h in range(HEADS_HERE):
        give_prefixes(1, h, later)
    for h in range(HEADS_HERE):
        state = whole_state(1, h, later)
        key_grad_ref[:, columns_of(h)] = (inner_key[h] + by_state_transposed(v[h], state)).astype(BF16)
        value_grad_ref[:, columns_of(h)] = (inner_value[h] + by_state(k[h], state)).astype(BF16)

    for h in range(HEADS_HERE):
        wait_sent(4, h, totals.at[1], n_y - 1)
        wait_sent(5, h, later, NZ - 1)


def store_kernel(*refs):
    sources, targets, sem = refs[:4], refs[4:8], refs[8]
    copies = [
        pltpu.make_async_copy(source, target, sem.at[i])
        for i, (source, target) in enumerate(zip(sources, targets))
    ]
    for copy in copies:
        copy.start()
    for copy in copies:
        copy.wait()


def shards(n_y, n_head, queries, key_vectors, value_vectors, out_gain, out_grad):
    part = HD // NZ
    by_head = (HEADS_HERE, TOK, HD)
    state = (HEADS_HERE, NZ, part, HD)
    anywhere = pl.BlockSpec(memory_space=pl.ANY)
    vmem = pl.BlockSpec(memory_space=pltpu.VMEM)
    results = pl.pallas_call(
        functools.partial(attention_kernel, n_y, n_head),
        out_shape=[pltpu.VMEM((TOK, HEADS_HERE * HD), BF16)] * 4,
        in_specs=[anywhere] * 5,
        out_specs=[vmem] * 4,
        scratch_shapes=[pltpu.VMEM(by_head, BF16)] * 4
        + [pltpu.VMEM((HEADS_HERE * HD,), BF16)]
        + [pltpu.VMEM(by_head, F32)] * 3
        + [
            pltpu.VMEM(by_head, BF16),
            pltpu.VMEM(state, F32),
            pltpu.VMEM(state, F32),
            pltpu.VMEM((2,) + state, F32),
            pltpu.VMEM((2,) + state, F32),
            pltpu.VMEM((2, HEADS_HERE, n_y, part, HD), F32),
            pltpu.VMEM((2,) + state, F32),
            pltpu.VMEM((2, HEADS_HERE, part, HD), F32),
            pltpu.VMEM((n_head, 8, HD), F32),
            pltpu.VMEM((8, HD), F32),
            pltpu.SemaphoreType.DMA((4, HEADS_HERE)),
            pltpu.SemaphoreType.DMA,
            pltpu.SemaphoreType.DMA((6, HEADS_HERE)),
            pltpu.SemaphoreType.DMA((6, HEADS_HERE)),
            pltpu.SemaphoreType.DMA,
            pltpu.SemaphoreType.DMA,
        ],
        compiler_params=pltpu.CompilerParams(
            collective_id=0, has_side_effects=True, vmem_limit_bytes=56 * 2**20
        ),
        name="attention",
    )(queries, key_vectors, value_vectors, out_grad, out_gain)
    whole = jax.ShapeDtypeStruct((TOK, HEADS_HERE * HD), BF16)
    return pl.pallas_call(
        store_kernel,
        out_shape=[whole] * 4,
        in_specs=[anywhere] * 4,
        out_specs=[anywhere] * 4,
        scratch_shapes=[pltpu.SemaphoreType.DMA((4,))],
        compiler_params=pltpu.CompilerParams(vmem_limit_bytes=2**20),
        name="store",
    )(*results)


def solution(mesh):
    n_y, n_head = mesh.shape["ctx"] // NZ, mesh.shape["head"]
    spec = P("ctx", "head")
    return jax.shard_map(
        functools.partial(shards, n_y, n_head),
        mesh=mesh,
        in_specs=(spec, spec, spec, P("head"), spec),
        out_specs=(spec,) * 4,
        check_vma=False,
    )
```

```python
import functools
import math

import jax
import jax.numpy as jnp
from jax import lax
from jax.experimental import pallas as pl
from jax.experimental.pallas import tpu as pltpu
from jax.sharding import PartitionSpec as P

HD = 128
TOK = 512
HEADS_HERE = 4
NZ = 8
SPLIT = 1
GROUPS = HEADS_HERE * SPLIT
EPSILON = 1e-05
SCALE = 1.0 / math.sqrt(HD)
MESH = pl.DeviceIdType.MESH
F32 = jnp.float32
BF16 = jnp.bfloat16


def product(a, b, contract):
    return lax.dot_general(a, b, ((contract[:1], contract[1:]), ((), ())), preferred_element_type=F32)


def rows_by_rows(a, b):
    return product(a, b, (1, 1))


def plain(a, b):
    return product(a, b, (1, 0))


def two_terms(state):
    high = state.astype(BF16)
    return high, (state - high.astype(F32)).astype(BF16)


def by_state(rows, state):
    high, low = two_terms(state)
    return plain(jnp.concatenate([rows, rows], axis=1), jnp.concatenate([high, low], axis=0)) * SCALE


def by_state_transposed(rows, state):
    high, low = two_terms(state)
    return rows_by_rows(jnp.concatenate([rows, rows], axis=1), jnp.concatenate([high, low], axis=1)) * SCALE


def score_block(a, b, keep):
    scores = rows_by_rows(a, b) * SCALE
    if keep is not None:
        scores = jnp.where(keep, scores, 0.0)
    return scores.astype(BF16)


def half_masks():
    half = TOK // 2
    rows = lax.broadcasted_iota(jnp.int32, (half, half), 0)
    columns = lax.broadcasted_iota(jnp.int32, (half, half), 1)
    return rows >= columns, rows <= columns


def sum_before(a, b, c, keep):
    half = TOK // 2
    first = plain(score_block(a[:half], b[:half], keep), c[:half])
    weights = jnp.concatenate([score_block(a[half:], b[:half], None), score_block(a[half:], b[half:], keep)], axis=1)
    return jnp.concatenate([first, plain(weights, c)], axis=0)


def sum_after(a, b, c, keep):
    half = TOK // 2
    weights = jnp.concatenate([score_block(a[:half], b[:half], keep), score_block(a[:half], b[half:], None)], axis=1)
    last = plain(score_block(a[half:], b[half:], keep), c[half:])
    return jnp.concatenate([plain(weights, c), last], axis=0)


def columns_of(h):
    return pl.ds(pl.multiple_of(h * HD, HD), HD)


def each(count, body):
    lax.fori_loop(0, count, lambda i, _: (body(i), 0)[1], 0)


def attention_kernel(
    n_y, n_head,
    q_hbm, k_hbm, v_hbm, g_hbm, gain_hbm,
    normed_ref, query_grad_ref, key_grad_ref, value_grad_ref,
    q, k, v, g, gain, gain_rows, q_turned, grad_in, squares, crossed, attended, inner_key, inner_value, do, prior, later,
    own, parts, totals, prefixes, total_out, sums, sums_out,
    in_sem, gain_sem, send_sem, recv_sem, sums_send, sums_recv,
):
    place, lane = lax.axis_index("ctx"), lax.axis_index("head")
    y, z = place // NZ, lax.rem(place, NZ)

    def along_z(other):
        return (y * NZ + other, lane)

    def along_y(other):
        return (other * NZ + z, lane)

    def along_head(other):
        return (place, other)

    def others(me, count):
        middle = count // 2
        steps = sorted(range(1, count), key=lambda step: (abs(step - middle), step))
        return [lax.rem(me + step, count) for step in steps]

    barrier = pltpu.get_barrier_semaphore()
    for me, count, device in ((z, NZ, along_z), (y, n_y, along_y), (lane, n_head, along_head)):
        for other in others(me, count):
            pl.semaphore_signal(barrier, inc=1, device_id=device(other), device_id_type=MESH)

    def load(which, h):
        source, target = ((k_hbm, k), (v_hbm, v), (q_hbm, q), (g_hbm, g))[which]
        return pltpu.make_async_copy(source.at[:, columns_of(h)], target.at[h], in_sem.at[which, h])

    gain_load = pltpu.make_async_copy(gain_hbm, gain, gain_sem)

    @functools.partial(each, HEADS_HERE)
    def load_keys(h):
        load(0, h).start()
        load(1, h).start()

    @functools.partial(each, HEADS_HERE)
    def load_queries(h):
        load(2, h).start()
        load(3, h).start()

    gain_load.start()

    def wait_all(phase, h, buffer, count):
        whole = buffer.at[h, pl.ds(0, count)]
        pltpu.make_async_remote_copy(
            src_ref=whole, dst_ref=whole, send_sem=send_sem.at[phase, h], recv_sem=recv_sem.at[phase, h],
            device_id=(place, lane), device_id_type=MESH,
        ).wait_recv()

    def wait_sent(phase, h, buffer, count):
        whole = buffer.at[h, pl.ds(0, count)]
        pltpu.make_async_remote_copy(
            src_ref=whole, dst_ref=whole, send_sem=send_sem.at[phase, h], recv_sem=recv_sem.at[phase, h],
            device_id=(place, lane), device_id_type=MESH,
        ).wait_send()

    def give_parts(scan, h):
        for other in others(z, NZ):
            pltpu.make_async_remote_copy(
                src_ref=own.at[scan, h, other], dst_ref=parts.at[scan, h, z],
                send_sem=send_sem.at[3 * scan, h], recv_sem=recv_sem.at[3 * scan, h],
                device_id=along_z(other), device_id_type=MESH,
            ).start()
        parts[scan, h, z] = own[scan, h, z]

    def give_totals(scan, h):
        wait_all(3 * scan, h, parts.at[scan], NZ - 1)
        order = list(range(NZ)) if scan == 0 else list(reversed(range(NZ)))
        running = parts[scan, h, order[0]]
        for at in order[1:]:
            running = running + parts[scan, h, at]
        total_out[scan, h] = running
        for other in others(y, n_y):
            pltpu.make_async_remote_copy(
                src_ref=total_out.at[scan, h], dst_ref=totals.at[scan, h, y],
                send_sem=send_sem.at[3 * scan + 1, h], recv_sem=recv_sem.at[3 * scan + 1, h],
                device_id=along_y(other), device_id_type=MESH,
            ).start()
        totals[scan, h, y] = running
        running = jnp.zeros(parts.shape[3:], F32)
        for at in order:
            prefixes[scan, h, at] = running
            running = running + parts[scan, h, at]

    def give_prefixes(scan, h, state):
        wait_all(3 * scan + 1, h, totals.at[scan], n_y - 1)
        offset = jnp.zeros(parts.shape[3:], F32)
        for at in range(n_y) if scan == 0 else reversed(range(n_y)):
            reached = at < y if scan == 0 else at > y
            offset = jnp.where(reached, offset + totals[scan, h, at], offset)
        for at in range(NZ):
            prefixes[scan, h, at] = prefixes[scan, h, at] + offset
        for other in others(z, NZ) if scan == 0 else others(z, NZ):
            pltpu.make_async_remote_copy(
                src_ref=prefixes.at[scan, h, other], dst_ref=state.at[h, z],
                send_sem=send_sem.at[3 * scan + 2, h], recv_sem=recv_sem.at[3 * scan + 2, h],
                device_id=along_z(other), device_id_type=MESH,
            ).start()
        state[h, z] = prefixes[scan, h, z]

    def whole_state(scan, h, state):
        for at in range(SPLIT):
            wait_all(3 * scan + 2, h * SPLIT + at, state, NZ - 1)
        return state[pl.ds(h * SPLIT, SPLIT)].reshape(HD, HD)

    below, above = half_masks()

    @functools.partial(each, HEADS_HERE)
    def key_value_state(h):
        load(0, h).wait()
        load(1, h).wait()
        own[0, pl.ds(h * SPLIT, SPLIT)] = product(k[h], v[h], (0, 0)).reshape((SPLIT,) + own.shape[2:])

    pl.semaphore_wait(barrier, NZ + n_y + n_head - 3)
    each(GROUPS, functools.partial(give_parts, 0))

    @functools.partial(each, HEADS_HERE)
    def inner_products(h):
        load(2, h).wait()
        load(3, h).wait()
        attended[h] = sum_before(q[h], k[h], v[h], below)

    def gain_row(h):
        return gain_rows[h]

    gain_load.wait()
    for h in range(HEADS_HERE):
        gain_rows[h] = gain[pl.ds(h * HD, HD)].astype(F32).reshape(1, HD)
    squares[...] = jnp.zeros((TOK, HD), F32)
    crossed[...] = jnp.zeros((TOK, HD), F32)

    @functools.partial(each, HEADS_HERE)
    def scaled_gradients(h):
        q_turned[h] = q[h].T
        grad_in[h] = gain_row(h) * g[h].astype(F32)

    each(GROUPS, functools.partial(give_totals, 0))
    each(GROUPS, lambda group: give_prefixes(0, group, prior))

    @functools.partial(each, HEADS_HERE)
    def outer_products(h):
        rows = attended[h] + by_state(q[h], whole_state(0, h, prior))
        attended[h] = rows
        squares[...] += rows * rows
        crossed[...] += grad_in[h] * rows

    ones = jnp.ones((8, 2 * HD), BF16)
    row = lax.broadcasted_iota(jnp.int32, (8, HD), 0)
    packed = jnp.zeros((8, HD), F32)
    for first, array in ((0, squares[...]), (4, crossed[...])):
        by_token = rows_by_rows(ones, jnp.concatenate(two_terms(array), axis=1))
        for r in range(4):
            packed = jnp.where(row == first + r, by_token[:, r * HD : (r + 1) * HD], packed)
    sums_out[...] = packed
    for other in others(lane, n_head):
        pltpu.make_async_remote_copy(
            src_ref=sums_out, dst_ref=sums.at[lane], send_sem=sums_send, recv_sem=sums_recv,
            device_id=along_head(other), device_id_type=MESH,
        ).start()
    sums[lane] = packed
    arrived = sums.at[pl.ds(0, n_head - 1)]
    sums_wait = pltpu.make_async_remote_copy(
        src_ref=arrived, dst_ref=arrived, send_sem=sums_send, recv_sem=sums_recv,
        device_id=(place, lane), device_id_type=MESH,
    )
    sums_wait.wait_recv()
    total = sums[0]
    for at in range(1, n_head):
        total = total + sums[at]
    mean = total * (1.0 / (n_head * HEADS_HERE * HD))
    inverse_rms = lax.rsqrt(mean + EPSILON)
    cubed = inverse_rms * inverse_rms * inverse_rms
    cross_factor = pltpu.roll(cubed, 4, 0) * mean
    factors = jnp.where(row < 4, inverse_rms, cross_factor)
    columns = jnp.concatenate([factors] * (HD // 8), axis=0).T
    rms_column = jnp.concatenate([columns[:, r : r + 1] for r in range(4)], axis=0)
    cross_column = jnp.concatenate([columns[:, 4 + r : 5 + r] for r in range(4)], axis=0)

    @functools.partial(each, HEADS_HERE)
    def query_state(h):
        do[h] = (rms_column * grad_in[h] - attended[h] * cross_column).astype(BF16)
        own[1, pl.ds(h * SPLIT, SPLIT)] = plain(q_turned[h], do[h]).reshape((SPLIT,) + own.shape[2:])
        for at in range(SPLIT):
            give_parts(1, h * SPLIT + at)

    @functools.partial(each, HEADS_HERE)
    def query_products(h):
        normed_ref[:, columns_of(h)] = (attended[h] * rms_column * gain_row(h)).astype(BF16)
        inner = sum_before(do[h], v[h], k[h], below)
        state = prior[pl.ds(h * SPLIT, SPLIT)].reshape(HD, HD)
        query_grad_ref[:, columns_of(h)] = (inner + by_state_transposed(do[h], state)).astype(BF16)

    @functools.partial(each, HEADS_HERE)
    def key_products(h):
        for at in range(SPLIT):
            give_totals(1, h * SPLIT + at)
        inner_key[h] = sum_after(v[h], do[h], q[h], above)
        inner_value[h] = sum_after(k[h], q[h], do[h], above)

    sums_wait.wait_send()

    @functools.partial(each, GROUPS)
    def earlier_sends(group):
        wait_sent(0, group, parts.at[0], NZ - 1)
        wait_sent(1, group, totals.at[0], n_y - 1)
        wait_sent(2, group, prior, NZ - 1)
        wait_sent(3, group, parts.at[1], NZ - 1)

    each(GROUPS, lambda group: give_prefixes(1, group, later))

    @functools.partial(each, HEADS_HERE)
    def key_and_value_grads(h):
        state = whole_state(1, h, later)
        key_grad_ref[:, columns_of(h)] = (inner_key[h] + by_state_transposed(v[h], state)).astype(BF16)
        value_grad_ref[:, columns_of(h)] = (inner_value[h] + by_state(k[h], state)).astype(BF16)

    @functools.partial(each, GROUPS)
    def last_sends(group):
        wait_sent(4, group, totals.at[1], n_y - 1)
        wait_sent(5, group, later, NZ - 1)


def store_kernel(*refs):
    sources, targets, sem = refs[:4], refs[4:8], refs[8]
    copies = [
        pltpu.make_async_copy(source, target, sem.at[i])
        for i, (source, target) in enumerate(zip(sources, targets))
    ]
    for copy in copies:
        copy.start()
    for copy in copies:
        copy.wait()


def shards(n_y, n_head, queries, key_vectors, value_vectors, out_gain, out_grad):
    part = HD // (NZ * SPLIT)
    by_head = (HEADS_HERE, TOK, HD)
    state = (GROUPS, NZ, part, HD)
    anywhere = pl.BlockSpec(memory_space=pl.ANY)
    vmem = pl.BlockSpec(memory_space=pltpu.VMEM)
    results = pl.pallas_call(
        functools.partial(attention_kernel, n_y, n_head),
        out_shape=[pltpu.VMEM((TOK, HEADS_HERE * HD), BF16)] * 4,
        in_specs=[anywhere] * 5,
        out_specs=[vmem] * 4,
        scratch_shapes=[pltpu.VMEM(by_head, BF16)] * 4
        + [pltpu.VMEM((HEADS_HERE * HD,), BF16), pltpu.VMEM((HEADS_HERE, 1, HD), F32)]
        + [pltpu.VMEM((HEADS_HERE, HD, TOK), BF16), pltpu.VMEM(by_head, F32)]
        + [pltpu.VMEM((TOK, HD), F32)] * 2
        + [pltpu.VMEM(by_head, F32)] * 3
        + [
            pltpu.VMEM(by_head, BF16),
            pltpu.VMEM(state, F32),
            pltpu.VMEM(state, F32),
            pltpu.VMEM((2,) + state, F32),
            pltpu.VMEM((2,) + state, F32),
            pltpu.VMEM((2, GROUPS, n_y, part, HD), F32),
            pltpu.VMEM((2,) + state, F32),
            pltpu.VMEM((2, GROUPS, part, HD), F32),
            pltpu.VMEM((n_head, 8, HD), F32),
            pltpu.VMEM((8, HD), F32),
            pltpu.SemaphoreType.DMA((4, HEADS_HERE)),
            pltpu.SemaphoreType.DMA,
            pltpu.SemaphoreType.DMA((6, GROUPS)),
            pltpu.SemaphoreType.DMA((6, GROUPS)),
            pltpu.SemaphoreType.DMA,
            pltpu.SemaphoreType.DMA,
        ],
        compiler_params=pltpu.CompilerParams(
            collective_id=0, has_side_effects=True, vmem_limit_bytes=58 * 2**20
        ),
        name="attention",
    )(queries, key_vectors, value_vectors, out_grad, out_gain)
    whole = jax.ShapeDtypeStruct((TOK, HEADS_HERE * HD), BF16)
    return pl.pallas_call(
        store_kernel,
        out_shape=[whole] * 4,
        in_specs=[anywhere] * 4,
        out_specs=[anywhere] * 4,
        scratch_shapes=[pltpu.SemaphoreType.DMA((4,))],
        compiler_params=pltpu.CompilerParams(vmem_limit_bytes=2**20),
        name="store",
    )(*results)


def solution(mesh):
    n_y, n_head = mesh.shape["ctx"] // NZ, mesh.shape["head"]
    spec = P("ctx", "head")
    return jax.shard_map(
        functools.partial(shards, n_y, n_head),
        mesh=mesh,
        in_specs=(spec, spec, spec, P("head"), spec),
        out_specs=(spec,) * 4,
        check_vma=False,
    )
```

```python
import functools
import math

import jax
import jax.numpy as jnp
from jax import lax
from jax.experimental import pallas as pl
from jax.experimental.pallas import tpu as pltpu
from jax.sharding import PartitionSpec as P

HD = 128
TOK = 512
HEADS_HERE = 4
NZ = 8
SPLIT = 1
GROUPS = HEADS_HERE * SPLIT
EPSILON = 1e-05
SCALE = 1.0 / math.sqrt(HD)
MESH = pl.DeviceIdType.MESH
F32 = jnp.float32
BF16 = jnp.bfloat16


def product(a, b, contract):
    return lax.dot_general(a, b, ((contract[:1], contract[1:]), ((), ())), preferred_element_type=F32)


def rows_by_rows(a, b):
    return product(a, b, (1, 1))


def plain(a, b):
    return product(a, b, (1, 0))


def two_terms(state):
    high = state.astype(BF16)
    return high, (state - high.astype(F32)).astype(BF16)


def by_state(rows, state):
    high, low = two_terms(state)
    return plain(jnp.concatenate([rows, rows], axis=1), jnp.concatenate([high, low], axis=0)) * SCALE


def by_state_transposed(rows, state):
    high, low = two_terms(state)
    return rows_by_rows(jnp.concatenate([rows, rows], axis=1), jnp.concatenate([high, low], axis=1)) * SCALE


def score_block(a, b, keep):
    scores = rows_by_rows(a, b) * SCALE
    if keep is not None:
        scores = jnp.where(keep, scores, 0.0)
    return scores.astype(BF16)


def half_masks():
    half = TOK // 2
    rows = lax.broadcasted_iota(jnp.int32, (half, half), 0)
    columns = lax.broadcasted_iota(jnp.int32, (half, half), 1)
    return rows >= columns, rows <= columns


def sum_before(a, b, c, keep):
    half = TOK // 2
    first = plain(score_block(a[:half], b[:half], keep), c[:half])
    weights = jnp.concatenate([score_block(a[half:], b[:half], None), score_block(a[half:], b[half:], keep)], axis=1)
    return jnp.concatenate([first, plain(weights, c)], axis=0)


def sum_after(a, b, c, keep):
    half = TOK // 2
    weights = jnp.concatenate([score_block(a[:half], b[:half], keep), score_block(a[:half], b[half:], None)], axis=1)
    last = plain(score_block(a[half:], b[half:], keep), c[half:])
    return jnp.concatenate([plain(weights, c), last], axis=0)


def columns_of(h):
    return pl.ds(pl.multiple_of(h * HD, HD), HD)


def each(count, body):
    lax.fori_loop(0, count, lambda i, _: (body(i), 0)[1], 0)


def attention_kernel(
    n_y, n_head,
    q_hbm, k_hbm, v_hbm, g_hbm, gain_hbm,
    normed_ref, query_grad_ref, key_grad_ref, value_grad_ref,
    q, k, v, g, gain, gain_rows, q_turned, grad_in, squares, crossed, attended, inner_key, inner_value, do, prior, later,
    own, parts, totals, prefixes, total_out, sums, sums_out,
    in_sem, gain_sem, send_sem, recv_sem, sums_send, sums_recv,
):
    place, lane = lax.axis_index("ctx"), lax.axis_index("head")
    y, z = place // NZ, lax.rem(place, NZ)

    def along_z(other):
        return (y * NZ + other, lane)

    def along_y(other):
        return (other * NZ + z, lane)

    def along_head(other):
        return (place, other)

    def others(me, count):
        middle = count // 2
        steps = sorted(range(1, count), key=lambda step: (abs(step - middle), step))
        return [lax.rem(me + step, count) for step in steps]

    barrier = pltpu.get_barrier_semaphore()
    for me, count, device in ((z, NZ, along_z), (y, n_y, along_y), (lane, n_head, along_head)):
        for other in others(me, count):
            pl.semaphore_signal(barrier, inc=1, device_id=device(other), device_id_type=MESH)

    def load(which, h):
        source, target = ((k_hbm, k), (v_hbm, v), (q_hbm, q), (g_hbm, g))[which]
        return pltpu.make_async_copy(source.at[:, columns_of(h)], target.at[h], in_sem.at[which, h])

    gain_load = pltpu.make_async_copy(gain_hbm, gain, gain_sem)

    @functools.partial(each, HEADS_HERE)
    def load_keys(h):
        load(0, h).start()
        load(1, h).start()

    @functools.partial(each, HEADS_HERE)
    def load_queries(h):
        load(2, h).start()
        load(3, h).start()

    gain_load.start()

    def wait_all(phase, h, buffer, count):
        whole = buffer.at[h, pl.ds(0, count)]
        pltpu.make_async_remote_copy(
            src_ref=whole, dst_ref=whole, send_sem=send_sem.at[phase, h], recv_sem=recv_sem.at[phase, h],
            device_id=(place, lane), device_id_type=MESH,
        ).wait_recv()

    def wait_sent(phase, h, buffer, count):
        whole = buffer.at[h, pl.ds(0, count)]
        pltpu.make_async_remote_copy(
            src_ref=whole, dst_ref=whole, send_sem=send_sem.at[phase, h], recv_sem=recv_sem.at[phase, h],
            device_id=(place, lane), device_id_type=MESH,
        ).wait_send()

    def give_parts(scan, h):
        for other in others(z, NZ):
            pltpu.make_async_remote_copy(
                src_ref=own.at[scan, h, other], dst_ref=parts.at[scan, h, z],
                send_sem=send_sem.at[3 * scan, h], recv_sem=recv_sem.at[3 * scan, h],
                device_id=along_z(other), device_id_type=MESH,
            ).start()
        parts[scan, h, z] = own[scan, h, z]

    def give_totals(scan, h):
        wait_all(3 * scan, h, parts.at[scan], NZ - 1)
        order = list(range(NZ)) if scan == 0 else list(reversed(range(NZ)))
        running = parts[scan, h, order[0]]
        for at in order[1:]:
            running = running + parts[scan, h, at]
        total_out[scan, h] = running
        for other in others(y, n_y):
            pltpu.make_async_remote_copy(
                src_ref=total_out.at[scan, h], dst_ref=totals.at[scan, h, y],
                send_sem=send_sem.at[3 * scan + 1, h], recv_sem=recv_sem.at[3 * scan + 1, h],
                device_id=along_y(other), device_id_type=MESH,
            ).start()
        totals[scan, h, y] = running
        running = jnp.zeros(parts.shape[3:], F32)
        for at in order:
            prefixes[scan, h, at] = running
            running = running + parts[scan, h, at]

    def give_prefixes(scan, h, state):
        wait_all(3 * scan + 1, h, totals.at[scan], n_y - 1)
        offset = jnp.zeros(parts.shape[3:], F32)
        for at in range(n_y) if scan == 0 else reversed(range(n_y)):
            reached = at < y if scan == 0 else at > y
            offset = jnp.where(reached, offset + totals[scan, h, at], offset)
        for at in range(NZ):
            prefixes[scan, h, at] = prefixes[scan, h, at] + offset
        for other in others(z, NZ) if scan == 0 else others(z, NZ):
            pltpu.make_async_remote_copy(
                src_ref=prefixes.at[scan, h, other], dst_ref=state.at[h, z],
                send_sem=send_sem.at[3 * scan + 2, h], recv_sem=recv_sem.at[3 * scan + 2, h],
                device_id=along_z(other), device_id_type=MESH,
            ).start()
        state[h, z] = prefixes[scan, h, z]

    def whole_state(scan, h, state):
        for at in range(SPLIT):
            wait_all(3 * scan + 2, h * SPLIT + at, state, NZ - 1)
        return state[pl.ds(h * SPLIT, SPLIT)].reshape(HD, HD)

    below, above = half_masks()

    @functools.partial(each, HEADS_HERE)
    def key_value_state(h):
        load(0, h).wait()
        load(1, h).wait()
        own[0, pl.ds(h * SPLIT, SPLIT)] = product(k[h], v[h], (0, 0)).reshape((SPLIT,) + own.shape[2:])

    pl.semaphore_wait(barrier, NZ + n_y + n_head - 3)
    each(GROUPS, functools.partial(give_parts, 0))

    @functools.partial(each, HEADS_HERE)
    def inner_products(h):
        load(2, h).wait()
        load(3, h).wait()
        attended[h] = sum_before(q[h], k[h], v[h], below)

    def gain_row(h):
        return gain_rows[h]

    gain_load.wait()
    for h in range(HEADS_HERE):
        gain_rows[h] = gain[pl.ds(h * HD, HD)].astype(F32).reshape(1, HD)
    squares[...] = jnp.zeros((TOK, HD), F32)
    crossed[...] = jnp.zeros((TOK, HD), F32)

    @functools.partial(each, HEADS_HERE)
    def scaled_gradients(h):
        q_turned[h] = q[h].T
        grad_in[h] = gain_row(h) * g[h].astype(F32)

    each(GROUPS, functools.partial(give_totals, 0))
    each(GROUPS, lambda group: give_prefixes(0, group, prior))

    @functools.partial(each, HEADS_HERE)
    def outer_products(h):
        rows = attended[h] + by_state(q[h], whole_state(0, h, prior))
        attended[h] = rows
        squares[...] += rows * rows
        crossed[...] += grad_in[h] * rows

    ones = jnp.ones((8, 2 * HD), BF16)
    row = lax.broadcasted_iota(jnp.int32, (8, HD), 0)
    packed = jnp.zeros((8, HD), F32)
    for first, array in ((0, squares[...]), (4, crossed[...])):
        by_token = rows_by_rows(ones, jnp.concatenate(two_terms(array), axis=1))
        for r in range(4):
            packed = jnp.where(row == first + r, by_token[:, r * HD : (r + 1) * HD], packed)
    sums_out[...] = packed
    for other in reversed(others(lane, n_head)):
        pltpu.make_async_remote_copy(
            src_ref=sums_out, dst_ref=sums.at[lane], send_sem=sums_send, recv_sem=sums_recv,
            device_id=along_head(other), device_id_type=MESH,
        ).start()
    sums[lane] = packed
    arrived = sums.at[pl.ds(0, n_head - 1)]
    sums_wait = pltpu.make_async_remote_copy(
        src_ref=arrived, dst_ref=arrived, send_sem=sums_send, recv_sem=sums_recv,
        device_id=(place, lane), device_id_type=MESH,
    )
    sums_wait.wait_recv()
    total = sums[0]
    for at in range(1, n_head):
        total = total + sums[at]
    mean = total * (1.0 / (n_head * HEADS_HERE * HD))
    inverse_rms = lax.rsqrt(mean + EPSILON)
    cubed = inverse_rms * inverse_rms * inverse_rms
    cross_factor = pltpu.roll(cubed, 4, 0) * mean
    factors = jnp.where(row < 4, inverse_rms, cross_factor)
    columns = jnp.concatenate([factors] * (HD // 8), axis=0).T
    rms_column = jnp.concatenate([columns[:, r : r + 1] for r in range(4)], axis=0)
    cross_column = jnp.concatenate([columns[:, 4 + r : 5 + r] for r in range(4)], axis=0)

    @functools.partial(each, HEADS_HERE)
    def query_state(h):
        do[h] = (rms_column * grad_in[h] - attended[h] * cross_column).astype(BF16)
        own[1, pl.ds(h * SPLIT, SPLIT)] = plain(q_turned[h], do[h]).reshape((SPLIT,) + own.shape[2:])
        for at in range(SPLIT):
            give_parts(1, h * SPLIT + at)

    @functools.partial(each, HEADS_HERE)
    def query_products(h):
        normed_ref[:, columns_of(h)] = (attended[h] * rms_column * gain_row(h)).astype(BF16)
        inner = sum_before(do[h], v[h], k[h], below)
        state = prior[pl.ds(h * SPLIT, SPLIT)].reshape(HD, HD)
        query_grad_ref[:, columns_of(h)] = (inner + by_state_transposed(do[h], state)).astype(BF16)

    sums_wait.wait_send()

    @functools.partial(each, GROUPS)
    def earlier_sends(group):
        wait_sent(0, group, parts.at[0], NZ - 1)
        wait_sent(1, group, totals.at[0], n_y - 1)
        wait_sent(2, group, prior, NZ - 1)

    def key_products(h):
        inner_key[h] = sum_after(v[h], do[h], q[h], above)
        inner_value[h] = sum_after(k[h], q[h], do[h], above)

    @functools.partial(each, HEADS_HERE)
    def totals_and_products(h):
        for at in range(SPLIT):
            give_totals(1, h * SPLIT + at)

        @pl.when(h < HEADS_HERE - 1)
        def products():
            key_products(h)

    each(GROUPS, lambda group: give_prefixes(1, group, later))
    each(1, lambda h: key_products(h + HEADS_HERE - 1))

    @functools.partial(each, GROUPS)
    def middle_sends(group):
        wait_sent(3, group, parts.at[1], NZ - 1)
        wait_sent(4, group, totals.at[1], n_y - 1)

    @functools.partial(each, HEADS_HERE)
    def key_and_value_grads(h):
        state = whole_state(1, h, later)
        key_grad_ref[:, columns_of(h)] = (inner_key[h] + by_state_transposed(v[h], state)).astype(BF16)
        value_grad_ref[:, columns_of(h)] = (inner_value[h] + by_state(k[h], state)).astype(BF16)

    @functools.partial(each, GROUPS)
    def last_sends(group):
        wait_sent(5, group, later, NZ - 1)


def store_kernel(*refs):
    sources, targets, sem = refs[:4], refs[4:8], refs[8]
    copies = [
        pltpu.make_async_copy(source, target, sem.at[i])
        for i, (source, target) in enumerate(zip(sources, targets))
    ]
    for copy in copies:
        copy.start()
    for copy in copies:
        copy.wait()


def shards(n_y, n_head, queries, key_vectors, value_vectors, out_gain, out_grad):
    part = HD // (NZ * SPLIT)
    by_head = (HEADS_HERE, TOK, HD)
    state = (GROUPS, NZ, part, HD)
    anywhere = pl.BlockSpec(memory_space=pl.ANY)
    vmem = pl.BlockSpec(memory_space=pltpu.VMEM)
    results = pl.pallas_call(
        functools.partial(attention_kernel, n_y, n_head),
        out_shape=[pltpu.VMEM((TOK, HEADS_HERE * HD), BF16)] * 4,
        in_specs=[anywhere] * 5,
        out_specs=[vmem] * 4,
        scratch_shapes=[pltpu.VMEM(by_head, BF16)] * 4
        + [pltpu.VMEM((HEADS_HERE * HD,), BF16), pltpu.VMEM((HEADS_HERE, 1, HD), F32)]
        + [pltpu.VMEM((HEADS_HERE, HD, TOK), BF16), pltpu.VMEM(by_head, F32)]
        + [pltpu.VMEM((TOK, HD), F32)] * 2
        + [pltpu.VMEM(by_head, F32)] * 3
        + [
            pltpu.VMEM(by_head, BF16),
            pltpu.VMEM(state, F32),
            pltpu.VMEM(state, F32),
            pltpu.VMEM((2,) + state, F32),
            pltpu.VMEM((2,) + state, F32),
            pltpu.VMEM((2, GROUPS, n_y, part, HD), F32),
            pltpu.VMEM((2,) + state, F32),
            pltpu.VMEM((2, GROUPS, part, HD), F32),
            pltpu.VMEM((n_head, 8, HD), F32),
            pltpu.VMEM((8, HD), F32),
            pltpu.SemaphoreType.DMA((4, HEADS_HERE)),
            pltpu.SemaphoreType.DMA,
            pltpu.SemaphoreType.DMA((6, GROUPS)),
            pltpu.SemaphoreType.DMA((6, GROUPS)),
            pltpu.SemaphoreType.DMA,
            pltpu.SemaphoreType.DMA,
        ],
        compiler_params=pltpu.CompilerParams(
            collective_id=0, has_side_effects=True, vmem_limit_bytes=58 * 2**20
        ),
        name="attention",
    )(queries, key_vectors, value_vectors, out_grad, out_gain)
    whole = jax.ShapeDtypeStruct((TOK, HEADS_HERE * HD), BF16)
    return pl.pallas_call(
        store_kernel,
        out_shape=[whole] * 4,
        in_specs=[anywhere] * 4,
        out_specs=[anywhere] * 4,
        scratch_shapes=[pltpu.SemaphoreType.DMA((4,))],
        compiler_params=pltpu.CompilerParams(vmem_limit_bytes=2**20),
        name="store",
    )(*results)


def solution(mesh):
    n_y, n_head = mesh.shape["ctx"] // NZ, mesh.shape["head"]
    spec = P("ctx", "head")
    return jax.shard_map(
        functools.partial(shards, n_y, n_head),
        mesh=mesh,
        in_specs=(spec, spec, spec, P("head"), spec),
        out_specs=(spec,) * 4,
        check_vma=False,
    )
```
